32 devices in a mesh: op: 16 (over z, y, x), sec: 2 (over core).
Axes of the slice: x: 2, y: 2, z: 4, core: 2. Of those that a mesh axis runs over, the one named last changes fastest.
Arguments:
- wavefunction: bfloat16 [2, 512, 512], P('sec', 'op'), may hold values from -6 to 6
- left_ops: bfloat16 [128, 512, 512], P(('op', 'sec')), may hold values from -0.25 to 0.25
- right_ops: bfloat16 [128, 512, 512], P(('op', 'sec')), may hold values from -0.25 to 0.25
- in_sector: int32 [128], P(('op', 'sec')), may hold values from 0 to 1
- counts: int32 [16, 2], replicated, may hold values from 1 to 4
Outputs:
- applied: bfloat16 [2, 512, 512], P('sec', 'op')
The draws below stay inside these ranges and needn't reach their ends.
Inputs may be any that keep to these rules, and one draw needn't show every extreme that they name: `counts`: a device's live terms are its first slots, as many as its count.
All inputs are finite; a program needn't handle non-finite values.
Results may differ from the reference program's by a relative error of at most 0.0049.
Values may be sent and summed in bfloat16 or wider, within the bound.
No kernel may reach another device: no remote copies, remote signals or barrier semaphores. Data moves between devices by JAX's collectives and lax.ppermute only.
A program may use at most 64 MiB of HBM per device.

```python
import jax
import jax.numpy as jnp
from jax import lax

K = 512
RL = 512
SLOTS = 4
SECT = 2
TERMS = 128
N_OP = 16
N_SEC = 2


def with_ends(drawn, own_key, smallest, largest):
    dims = drawn.shape
    place = [jax.random.randint(jax.random.fold_in(own_key, axis), (), 0, dims[axis]) for axis in range(len(dims))]
    drawn = drawn.at[tuple(place)].set(smallest)
    longest = dims.index(max(dims))
    place[longest] = (place[longest] + 1) % dims[longest]
    return drawn.at[tuple(place)].set(largest)


def levels(stream_key, dims, shards, smallest, top_value):
    level, own = 1.0, jax.random.fold_in(stream_key, 6)
    for position, parts in shards:
        steps = jnp.exp(jax.random.uniform(jax.random.fold_in(own, position), (parts,), jnp.float32, smallest / len(shards), top_value / len(shards)))
        level = level * jnp.repeat(steps, dims[position] // parts).reshape([-1 if axis == position else 1 for axis in range(len(dims))])
    return level


def scatter_about(rng, extent, scale, most, cuts=(), held_as=jnp.bfloat16):
    array = scale * jax.random.normal(rng, extent, jnp.float32)
    if cuts:
        array = array * levels(rng, extent, cuts, -0.22, 0.18)
    return jnp.clip(array, -most, most).astype(held_as)


def setup_inputs(seed: int = 0) -> dict:
    seeds = jax.random.split(jax.random.key(seed), 6)
    wavefunction = scatter_about(seeds[0], (SECT, K, K), 1.0, 6.0, ((0, 2), (1, 16)))
    left_ops = scatter_about(seeds[1], (TERMS, RL, K), K ** -0.5, 0.25, ((0, 32),))
    right_ops = scatter_about(seeds[2], (TERMS, K, K), K ** -0.5, 0.25, ((0, 32),))
    in_sector = with_ends(jax.random.randint(seeds[3], (TERMS,), 0, SECT), jax.random.fold_in(seeds[3], 1), 0, SECT - 1).astype(jnp.int32)
    counts = with_ends(jax.random.randint(seeds[4], (N_OP, N_SEC), 1, SLOTS + 1), jax.random.fold_in(seeds[4], 1), 1, SLOTS).astype(jnp.int32)
    return {"wavefunction": wavefunction, "left_ops": left_ops, "right_ops": right_ops, "in_sector": in_sector, "counts": counts}


def reference(wavefunction, left_ops, right_ops, in_sector, counts):
    positions = jnp.arange(TERMS, dtype=jnp.int32)
    device = positions // SLOTS
    slot_index = positions % SLOTS
    owner_op = device // N_SEC
    owner_sec = device % N_SEC
    living = slot_index < counts[owner_op, owner_sec]

    def accumulate(summed, pieces):
        left_block, right_block, sector, target, alive = pieces

        def add_term(current):
            sector_block = lax.dynamic_index_in_dim(wavefunction, sector, 0, keepdims=False)
            halfway = jnp.dot(left_block, sector_block, preferred_element_type=jnp.float32).astype(jnp.bfloat16)
            product = lax.dot_general(halfway, right_block, (((1,), (1,)), ((), ())), preferred_element_type=jnp.float32)
            previous = lax.dynamic_index_in_dim(current, target, 0, keepdims=False)
            return lax.dynamic_update_index_in_dim(current, previous + product, target, 0)

        def keep_sum(current):
            return current

        return lax.cond(alive, add_term, keep_sum, summed), None

    initial = jnp.zeros((SECT, RL, K), jnp.float32)
    summed, unused = lax.scan(accumulate, initial, (left_ops, right_ops, in_sector, owner_sec.astype(jnp.int32), living))
    factor = (N_OP * SLOTS) ** -0.5
    return (summed * factor).astype(jnp.bfloat16)
```

```python
import functools

import jax
import jax.numpy as jnp
from jax import lax
from jax.experimental import pallas as pl
from jax.experimental.pallas import tpu as pltpu
from jax.sharding import PartitionSpec as P


def exchange(value, axis, mask):
    size = lax.axis_size(axis)
    return lax.ppermute(value, axis, [(i, i ^ mask) for i in range(size)])


def spread(position, masks):
    return sum(mask for bit, mask in enumerate(masks) if position >> bit & 1)


def unfold(gathered, place, masks):
    bits = len(masks)
    folded = gathered.reshape((2,) * bits + (-1, gathered.shape[1]))
    for bit, mask in enumerate(masks):
        there = (place & mask) != 0
        folded = jnp.where(there, jnp.flip(folded, bits - 1 - bit), folded)
    return folded.transpose(tuple(range(bits))[::-1] + (bits, bits + 1)).reshape(gathered.shape)


def terms_kernel(blocks, sizes, home_ref, away_ref, sector_ref, count_ref, *refs):
    sectors, pieces = sizes
    piece_refs, refs = refs[: sectors * pieces], refs[sectors * pieces :]
    left_ref, right_ref, keep_ref, send_ref, wave, ordered = refs
    for sector in range(sectors):
        first = 0
        for piece in range(pieces):
            ref = piece_refs[sector * pieces + piece]
            for part in range(ref.shape[0] // blocks):
                start = pl.multiple_of(away_ref[first] * blocks, blocks)
                wave[home_ref[home_ref.shape[0] - sectors + sector], pl.ds(start, blocks), :] = ref[
                    part * blocks : (part + 1) * blocks, :
                ]
                first += 1
    slots = left_ref.shape[0]
    total = None
    for slot in range(slots):
        halfway = jnp.dot(
            left_ref[slot], wave[sector_ref[slot]], preferred_element_type=jnp.float32
        ).astype(jnp.bfloat16)
        halfway = jnp.where(slot < count_ref[0], halfway, jnp.zeros_like(halfway))
        product = lax.dot_general(
            halfway, right_ref[slot], (((1,), (1,)), ((), ())), preferred_element_type=jnp.float32
        )
        total = product if total is None else total + product
    share = keep_ref.shape[0] * 2 // (home_ref.shape[0] - sectors)
    for block in range(home_ref.shape[0] - sectors):
        start = pl.multiple_of(home_ref[block] * share, share)
        ordered[pl.ds(start, share), :] = total[block * share : (block + 1) * share, :]
    half = keep_ref.shape[0]
    keep_ref[...] = ordered[:half, :]
    send_ref[...] = ordered[half:, :].astype(jnp.bfloat16)


def shards(wavefunction, left_ops, right_ops, in_sector, counts):
    op_devices, sec_devices = lax.axis_size("op"), lax.axis_size("sec")
    op_place, sec_place = lax.axis_index("op"), lax.axis_index("sec")
    slots, left_rows, order = left_ops.shape
    near = [1 << bit for bit in range(op_devices.bit_length() - 1)]
    far = near[::-1]

    held = wavefunction[0]
    pieces = [held]
    for step, mask in enumerate(far):
        arrived = exchange(held, "op", mask)
        pieces.append(arrived)
        if step < len(far) - 1:
            held = jnp.concatenate([held, arrived], axis=0)
    by_sector = [pieces]
    for mask in range(1, sec_devices):
        by_sector.append([exchange(piece, "sec", mask) for piece in pieces])

    away = op_place ^ jnp.array([spread(p, far) for p in range(op_devices)], jnp.int32)
    inverse = [0] * op_devices
    for position in range(op_devices):
        inverse[spread(position, near[::-1])] = position
    home = jnp.array(inverse, jnp.int32)[op_place ^ jnp.arange(op_devices)]
    places = sec_place ^ jnp.arange(sec_devices, dtype=jnp.int32)
    home = jnp.concatenate([home, places])
    count = lax.dynamic_slice(counts, (op_place, sec_place), (1, 1))[0]

    blocks = held.shape[0] * 2 // op_devices
    if blocks % 16:
        by_sector = [[unfold(jnp.concatenate(group, axis=0), op_place, far)] for group in by_sector]
        blocks, away = order, jnp.zeros((1,), jnp.int32)
    flat = [piece for group in by_sector for piece in group]
    smem, vmem = pl.BlockSpec(memory_space=pltpu.SMEM), pl.BlockSpec(memory_space=pltpu.VMEM)
    half = left_rows // 2
    keep, send = pl.pallas_call(
        functools.partial(terms_kernel, blocks, (sec_devices, len(by_sector[0]))),
        out_shape=(
            jax.ShapeDtypeStruct((half, order), jnp.float32),
            jax.ShapeDtypeStruct((half, order), jnp.bfloat16),
        ),
        in_specs=[smem] * 4 + [vmem] * (len(flat) + 2),
        out_specs=(vmem, vmem),
        scratch_shapes=[
            pltpu.VMEM((sec_devices, order, order), jnp.bfloat16),
            pltpu.VMEM((left_rows, order), jnp.float32),
        ],
        compiler_params=pltpu.CompilerParams(vmem_limit_bytes=32 * 2**20),
        cost_estimate=pl.CostEstimate(
            flops=4 * slots * left_rows * order * order,
            bytes_accessed=4 * slots * left_rows * order,
            transcendentals=0,
        ),
    )(home, away, in_sector, count, *flat, left_ops, right_ops)

    for mask in near[:-1]:
        arrived = exchange(send, "op", mask).astype(jnp.float32)
        half //= 2
        send = (keep[half:] + arrived[half:]).astype(jnp.bfloat16)
        keep = keep[:half] + arrived[:half]
    shares = keep + exchange(send, "op", near[-1]).astype(jnp.float32)
    factor = (op_devices * slots) ** (-0.5)
    return (shares * factor).astype(jnp.bfloat16)[None]


def solution(mesh):
    placed = (
        P("sec", "op", None),
        P(("op", "sec"), None, None),
        P(("op", "sec"), None, None),
        P(("op", "sec")),
        P(),
    )
    return jax.shard_map(
        shards, mesh=mesh, in_specs=placed, out_specs=P("sec", "op", None), check_vma=False
    )
```

```python
import functools

import jax
import jax.numpy as jnp
from jax import lax
from jax.experimental import pallas as pl
from jax.experimental.pallas import tpu as pltpu
from jax.sharding import PartitionSpec as P

F32, BF16 = jnp.float32, jnp.bfloat16
SMEM = pl.BlockSpec(memory_space=pltpu.SMEM)
VMEM = pl.BlockSpec(memory_space=pltpu.VMEM)
HBM = pl.BlockSpec(memory_space=pl.ANY)


def exchange(value, axis, mask):
    size = lax.axis_size(axis)
    return lax.ppermute(value, axis, [(i, i ^ mask) for i in range(size)])


def spread(position, masks):
    return sum(mask for bit, mask in enumerate(masks) if position >> bit & 1)


def load_kernel(*refs):
    count = len(refs) // 2
    sources, places, sems = refs[:count], refs[count : 2 * count], refs[2 * count]
    copies = [
        pltpu.make_async_copy(source, place, sems.at[i])
        for i, (source, place) in enumerate(zip(sources, places))
    ]
    for copy in copies:
        copy.start()
    for copy in copies:
        copy.wait()


def load(*arrays):
    size = sum(array.size * array.dtype.itemsize for array in arrays)
    return pl.pallas_call(
        load_kernel,
        out_shape=tuple(jax.ShapeDtypeStruct(a.shape, a.dtype) for a in arrays),
        in_specs=[HBM] * len(arrays),
        out_specs=(VMEM,) * len(arrays),
        scratch_shapes=[pltpu.SemaphoreType.DMA((len(arrays),))],
        compiler_params=pltpu.CompilerParams(vmem_limit_bytes=16 * 2**20),
        cost_estimate=pl.CostEstimate(flops=0, bytes_accessed=2 * size, transcendentals=0),
    )(*arrays)


def row_sums(distances, rows, place, count, sector_ref, left_ref, right_ref, wave_ref):
    starts = [pl.multiple_of((place ^ distance) * rows, rows) for distance in distances]
    total = None
    for slot in range(left_ref.shape[0]):
        left = jnp.concatenate([left_ref[slot, pl.ds(start, rows), :] for start in starts], axis=0)
        halfway = jnp.dot(left, wave_ref[sector_ref[slot]], preferred_element_type=F32).astype(BF16)
        halfway = jnp.where(slot < count, halfway, jnp.zeros_like(halfway))
        product = lax.dot_general(
            halfway, right_ref[slot], (((1,), (1,)), ((), ())), preferred_element_type=F32
        )
        total = product if total is None else total + product
    return total


def far_kernel(gathered, scattered, near, rows, sector_ref, counts_ref, *refs):
    pieces, (left_ref, right_ref, wave_ref, first_ref, second_ref) = refs[:-5], refs[-5:]
    place, sector = lax.axis_index("op"), lax.axis_index("sec")
    distances = [gather ^ quarter for quarter in (0, near[0], near[1], near[0] ^ near[1]) for gather in gathered]
    row = 0
    for ref in pieces:
        away, first = divmod(row, len(distances) * rows)
        for part in range(ref.shape[0] // rows):
            start = pl.multiple_of((place ^ distances[first // rows + part]) * rows, rows)
            wave_ref[sector ^ away, pl.ds(start, rows), :] = ref[part * rows : (part + 1) * rows, :]
        row += ref.shape[0]
    total = row_sums(
        [distance ^ near[0] ^ near[1] for distance in scattered],
        rows, place, counts_ref[place, sector], sector_ref, left_ref, right_ref, wave_ref,
    ).astype(BF16)
    half = first_ref.shape[0]
    first_ref[...], second_ref[...] = total[:half, :], total[half:, :]


def near_kernel(scattered, near, rows, sector_ref, counts_ref, left_ref, right_ref, wave_ref, *sums):
    place, sector = lax.axis_index("op"), lax.axis_index("sec")
    total = row_sums(
        [distance ^ quarter for quarter in (0, *near) for distance in scattered],
        rows, place, counts_ref[place, sector], sector_ref, left_ref, right_ref, wave_ref,
    )
    row = 0
    for ref in sums:
        ref[...] = total[row : row + ref.shape[0], :].astype(ref.dtype)
        row += ref.shape[0]


def by_neighbours(wavefunction, left_ops, right_ops, in_sector, counts):
    op_devices, sec_devices = lax.axis_size("op"), lax.axis_size("sec")
    slots, left_rows, order = left_ops.shape
    masks = [1 << bit for bit in range(op_devices.bit_length() - 1)]
    near, line = masks[:2], masks[2:]
    rows, wide = left_rows // op_devices, left_rows // 4
    gathered = [spread(p, line[::-1]) for p in range(op_devices // 4)]
    scattered = gathered
    barrier = lax.optimization_barrier

    def to_sectors(piece):
        return [exchange(piece, "sec", away) for away in range(1, sec_devices)]

    left, right, held = load(left_ops, right_ops, wavefunction[0])
    for step, mask in enumerate(line[::-1]):
        arrived = exchange(wavefunction[0] if step == 0 else held, "op", mask)
        held = jnp.concatenate([held, arrived], axis=0)
    half = held.shape[0] // 2
    beside = [exchange(held, "op", mask) for mask in near]
    others = [to_sectors(held)]
    beside, others = barrier((beside, others))
    diagonal = [exchange(beside[1][:half], "op", near[0]), exchange(beside[0][half:], "op", near[1])]
    others.append(to_sectors(jnp.concatenate(beside, axis=0)))
    diagonal, others = barrier((diagonal, others))
    others.append(to_sectors(jnp.concatenate(diagonal, axis=0)))
    pieces = [held, *beside, *diagonal]
    for away in range(sec_devices - 1):
        pieces += [group[away] for group in others]

    def cost(part):
        return pl.CostEstimate(
            flops=int(4 * slots * left_rows * order * order * part),
            bytes_accessed=int(4 * slots * left_rows * order),
            transcendentals=0,
        )

    params = pltpu.CompilerParams(vmem_limit_bytes=24 * 2**20)
    wave, *sends = pl.pallas_call(
        functools.partial(far_kernel, gathered, scattered, near, rows),
        out_shape=(
            jax.ShapeDtypeStruct((sec_devices, order, order), BF16),
            jax.ShapeDtypeStruct((wide // 2, order), BF16),
            jax.ShapeDtypeStruct((wide // 2, order), BF16),
        ),
        in_specs=[SMEM] * 2 + [VMEM] * (len(pieces) + 2),
        out_specs=(VMEM,) * 3,
        compiler_params=params,
        cost_estimate=cost(0.25),
    )(in_sector, counts, *pieces, left, right)

    passed = [exchange(send, "op", mask) for send, mask in zip(sends, near)]
    own, x_first, x_second, y_first, y_second = pl.pallas_call(
        functools.partial(near_kernel, scattered, near, rows),
        out_shape=(
            jax.ShapeDtypeStruct((wide, order), F32),
            jax.ShapeDtypeStruct((wide // 2, order), BF16),
            jax.ShapeDtypeStruct((wide // 2, order), F32),
            jax.ShapeDtypeStruct((wide // 2, order), F32),
            jax.ShapeDtypeStruct((wide // 2, order), BF16),
        ),
        in_specs=[SMEM] * 2 + [VMEM] * 3,
        out_specs=(VMEM,) * 5,
        compiler_params=params,
        cost_estimate=cost(0.75),
    )(in_sector, counts, left, right, wave)
    to_x = jnp.concatenate([x_first, (x_second + passed[1].astype(F32)).astype(BF16)], axis=0)
    to_y = jnp.concatenate([(y_first + passed[0].astype(F32)).astype(BF16), y_second], axis=0)
    keep = own + exchange(to_x, "op", near[0]).astype(F32) + exchange(to_y, "op", near[1]).astype(F32)
    for mask in line:
        half = keep.shape[0] // 2
        keep = keep[:half] + exchange(keep[half:].astype(BF16), "op", mask).astype(F32)
    factor = (op_devices * slots) ** (-0.5)
    return (keep * factor).astype(BF16)[None]


def by_collectives(wavefunction, left_ops, right_ops, in_sector, counts):
    slots, left_rows, order = left_ops.shape
    by_rows = lax.all_gather(wavefunction, "op", axis=1, tiled=True)
    gathered = lax.all_gather(by_rows, "sec", axis=0, tiled=True)

    def term(slot, summed):
        halfway = jnp.dot(left_ops[slot], gathered[in_sector[slot]], preferred_element_type=F32)
        product = lax.dot_general(
            halfway.astype(BF16), right_ops[slot], (((1,), (1,)), ((), ())), preferred_element_type=F32
        )
        return summed + product

    count = counts[lax.axis_index("op"), lax.axis_index("sec")]
    summed = lax.fori_loop(0, count, term, jnp.zeros((left_rows, order), F32))
    shares = lax.psum_scatter(summed, "op", scatter_dimension=0, tiled=True)
    factor = (lax.axis_size("op") * slots) ** (-0.5)
    return (shares * factor).astype(BF16)[None]


def shards(wavefunction, left_ops, right_ops, in_sector, counts):
    op_devices, sec_devices = lax.axis_size("op"), lax.axis_size("sec")
    powers = all(size & (size - 1) == 0 for size in (op_devices, sec_devices))
    tiles = left_ops.shape[1] % (16 * op_devices) == 0 and left_ops.shape[1] == left_ops.shape[2]
    body = by_neighbours if powers and tiles and op_devices >= 8 else by_collectives
    return body(wavefunction, left_ops, right_ops, in_sector, counts)


def solution(mesh):
    placed = (
        P("sec", "op", None),
        P(("op", "sec"), None, None),
        P(("op", "sec"), None, None),
        P(("op", "sec")),
        P(),
    )
    return jax.shard_map(
        shards, mesh=mesh, in_specs=placed, out_specs=P("sec", "op", None), check_vma=False
    )
```

```python
import functools

import jax
import jax.numpy as jnp
from jax import lax
from jax.experimental import pallas as pl
from jax.experimental.pallas import tpu as pltpu
from jax.sharding import PartitionSpec as P

F32, BF16 = jnp.float32, jnp.bfloat16
SMEM = pl.BlockSpec(memory_space=pltpu.SMEM)
VMEM = pl.BlockSpec(memory_space=pltpu.VMEM)
HBM = pl.BlockSpec(memory_space=pltpu.HBM)


def exchange(value, axis, mask):
    size = lax.axis_size(axis)
    return lax.ppermute(value, axis, [(i, i ^ mask) for i in range(size)])


def spread(position, masks):
    return sum(mask for bit, mask in enumerate(masks) if position >> bit & 1)


def load_kernel(source, place, sem):
    copy = pltpu.make_async_copy(source, place, sem)
    copy.start()
    copy.wait()


def load(array):
    size = array.size * array.dtype.itemsize
    return pl.pallas_call(
        load_kernel,
        out_shape=jax.ShapeDtypeStruct(array.shape, array.dtype),
        in_specs=[HBM],
        out_specs=VMEM,
        scratch_shapes=[pltpu.SemaphoreType.DMA],
        compiler_params=pltpu.CompilerParams(vmem_limit_bytes=2**20),
        cost_estimate=pl.CostEstimate(flops=0, bytes_accessed=2 * size, transcendentals=0),
    )(array)


def terms_kernel(order, sector_ref, counts_ref, left_hbm, right_hbm, *refs):
    waves, (sum_ref, wave, left_ref, right_ref, left_sem, right_sem) = refs[:-6], refs[-6:]
    slots, rows = left_ref.shape[0], left_ref.shape[1] // len(order)
    lefts = [pltpu.make_async_copy(left_hbm.at[t], left_ref.at[t], left_sem.at[t]) for t in range(slots)]
    rights = [pltpu.make_async_copy(right_hbm.at[t], right_ref.at[t], right_sem.at[t]) for t in range(slots)]
    for left, right in zip(lefts, rights):
        left.start()
        right.start()
    for away, ref in enumerate(waves):
        for place, block in enumerate(order):
            group, part = divmod(place * rows, ref.shape[1])
            wave[away, block * rows : (block + 1) * rows, :] = ref[group, part : part + rows, :]
    sector = lax.axis_index("sec")
    count = counts_ref[lax.axis_index("op"), sector]
    total = None
    for slot in range(slots):
        away = lax.rem(sector - sector_ref[slot] + len(waves), len(waves))
        lefts[slot].wait()
        halfway = jnp.dot(left_ref[slot], wave[away], preferred_element_type=F32).astype(BF16)
        halfway = jnp.where(slot < count, halfway, jnp.zeros_like(halfway))
        rights[slot].wait()
        product = lax.dot_general(
            halfway, right_ref[slot], (((1,), (1,)), ((), ())), preferred_element_type=F32
        )
        total = product if total is None else total + product
    for place, block in enumerate(order):
        group, part = divmod(place * rows, sum_ref.shape[1])
        sum_ref[group, part : part + rows, :] = total[block * rows : (block + 1) * rows, :].astype(BF16)


def shards(wavefunction, left_ops, right_ops, in_sector, counts):
    op_devices, sec_devices = lax.axis_size("op"), lax.axis_size("sec")
    op_place = lax.axis_index("op")
    slots, left_rows, order = left_ops.shape
    near = min(8, op_devices) if op_devices & (op_devices - 1) == 0 else op_devices
    far = [near << bit for bit in range((op_devices // near).bit_length() - 1)]
    groups = [[far_place * near + i for i in range(near)] for far_place in range(op_devices // near)]
    blocks = [i + spread(p, far[::-1]) for i in range(near) for p in range(op_devices // near)]

    held = wavefunction[0]
    for step, mask in enumerate(far[::-1]):
        arrived = exchange(held, "op", mask)
        if step == 0:
            held = load(held)
        there = (op_place & mask) != 0
        held = jnp.concatenate(
            [jnp.where(there, arrived, held), jnp.where(there, held, arrived)], axis=0
        )
    held = jnp.broadcast_to(held[None], (near, *held.shape))
    gathered = [lax.all_to_all(held, "op", 0, 0, axis_index_groups=groups)]
    for away in range(1, sec_devices):
        turn = [(i, (i + away) % sec_devices) for i in range(sec_devices)]
        gathered.append(lax.ppermute(gathered[0], "sec", turn))

    summed = pl.pallas_call(
        functools.partial(terms_kernel, blocks),
        out_shape=jax.ShapeDtypeStruct((near, left_rows // near, order), BF16),
        in_specs=[SMEM] * 2 + [HBM] * 2 + [VMEM] * sec_devices,
        out_specs=VMEM,
        scratch_shapes=[
            pltpu.VMEM((sec_devices, order, order), BF16),
            pltpu.VMEM(left_ops.shape, BF16),
            pltpu.VMEM(right_ops.shape, BF16),
            pltpu.SemaphoreType.DMA((slots,)),
            pltpu.SemaphoreType.DMA((slots,)),
        ],
        compiler_params=pltpu.CompilerParams(vmem_limit_bytes=51 * 2**20),
        cost_estimate=pl.CostEstimate(
            flops=4 * slots * left_rows * order * order,
            bytes_accessed=4 * slots * left_rows * order,
            transcendentals=0,
        ),
    )(in_sector, counts, left_ops, right_ops, *gathered)

    parts = lax.all_to_all(summed, "op", 0, 0, axis_index_groups=groups)
    keep = jnp.sum(parts.astype(F32), axis=0)
    for mask in far:
        half = keep.shape[0] // 2
        there = (op_place & mask) != 0
        send = jnp.where(there, keep[:half], keep[half:]).astype(BF16)
        keep = jnp.where(there, keep[half:], keep[:half]) + exchange(send, "op", mask).astype(F32)
    factor = (op_devices * slots) ** (-0.5)
    return (keep * factor).astype(BF16)[None]


def solution(mesh):
    placed = (
        P("sec", "op", None),
        P(("op", "sec"), None, None),
        P(("op", "sec"), None, None),
        P(("op", "sec")),
        P(),
    )
    return jax.shard_map(
        shards, mesh=mesh, in_specs=placed, out_specs=P("sec", "op", None), check_vma=False
    )
```

```python
import functools

import jax
import jax.numpy as jnp
from jax import lax
from jax.experimental import pallas as pl
from jax.experimental.pallas import tpu as pltpu
from jax.sharding import PartitionSpec as P

F32, BF16 = jnp.float32, jnp.bfloat16
SMEM = pl.BlockSpec(memory_space=pltpu.SMEM)
VMEM = pl.BlockSpec(memory_space=pltpu.VMEM)
HBM = pl.BlockSpec(memory_space=pltpu.HBM)


def exchange(value, axis, mask):
    size = lax.axis_size(axis)
    return lax.ppermute(value, axis, [(i, i ^ mask) for i in range(size)])


def spread(position, masks):
    return sum(mask for bit, mask in enumerate(masks) if position >> bit & 1)


def costs(bytes_accessed, flops=0):
    return pl.CostEstimate(flops=flops, bytes_accessed=bytes_accessed, transcendentals=0)


def load_kernel(source, place, sem):
    copy = pltpu.make_async_copy(source, place, sem)
    copy.start()
    copy.wait()


def load(array):
    return pl.pallas_call(
        load_kernel,
        out_shape=jax.ShapeDtypeStruct(array.shape, array.dtype),
        in_specs=[HBM],
        out_specs=VMEM,
        scratch_shapes=[pltpu.SemaphoreType.DMA],
        compiler_params=pltpu.CompilerParams(vmem_limit_bytes=2**20),
        cost_estimate=costs(2 * array.size * array.dtype.itemsize),
    )(array)


def in_order(order, rows, source, place):
    for position, block in enumerate(order):
        group, part = divmod(position * rows, source.shape[1])
        place[block * rows : (block + 1) * rows, :] = source[group, part : part + rows, :]


def scalars_kernel(sectors, sector_ref, counts_ref, scalars_ref):
    sector = lax.axis_index("sec")
    count = counts_ref[sector, lax.axis_index("op")]
    for slot in range(scalars_ref.shape[0]):
        away = lax.rem(sector - sector_ref[slot] + sectors, sectors)
        scalars_ref[slot] = jnp.where(slot < count, away, -1)


def terms_kernel(order, scalars_ref, left_ref, right_hbm, own_ref, *refs):
    others, (sum_ref, wave, right_ref, sems) = refs[:-4], refs[-4:]
    slots, rows = left_ref.shape[0], left_ref.shape[1] // len(order)
    copies = [pltpu.make_async_copy(right_hbm.at[t], right_ref.at[t], sems.at[t]) for t in range(slots)]
    for copy in copies:
        copy.start()
    wave[0] = own_ref[...]
    for away, ref in enumerate(others):
        in_order(order, rows, ref, wave.at[away + 1])
    halfways = []
    for slot in range(slots):
        away = scalars_ref[slot]
        halfway = jnp.dot(left_ref[slot], wave[jnp.maximum(away, 0)], preferred_element_type=F32).astype(BF16)
        halfways.append(jnp.where(away >= 0, halfway, jnp.zeros_like(halfway)))
    total = None
    for slot in range(slots):
        copies[slot].wait()
        product = lax.dot_general(
            halfways[slot], right_ref[slot], (((1,), (1,)), ((), ())), preferred_element_type=F32
        )
        total = product if total is None else total + product
    for place, block in enumerate(order):
        group, part = divmod(place * rows, sum_ref.shape[1])
        sum_ref[group, part : part + rows, :] = total[block * rows : (block + 1) * rows, :].astype(BF16)


def shards(wavefunction, left_ops, right_ops, in_sector, counts):
    op_devices, sec_devices = lax.axis_size("op"), lax.axis_size("sec")
    op_place = lax.axis_index("op")
    slots, left_rows, order = left_ops.shape
    near = min(8, op_devices) if op_devices & (op_devices - 1) == 0 else op_devices
    far = [near << bit for bit in range((op_devices // near).bit_length() - 1)]
    groups = [[far_place * near + i for i in range(near)] for far_place in range(op_devices // near)]
    blocks = [i + spread(p, far[::-1]) for i in range(near) for p in range(op_devices // near)]

    scalars = pl.pallas_call(
        functools.partial(scalars_kernel, sec_devices),
        out_shape=jax.ShapeDtypeStruct((slots,), jnp.int32),
        in_specs=[SMEM] * 2,
        out_specs=SMEM,
        compiler_params=pltpu.CompilerParams(vmem_limit_bytes=2**20),
    )(in_sector, counts.T)
    held = wavefunction[0]
    for step, mask in enumerate(far[::-1]):
        arrived = exchange(held, "op", mask)
        if step == 0:
            held, scalars = lax.optimization_barrier((load(held), scalars))
        there = (op_place & mask) != 0
        held = jnp.concatenate(
            [jnp.where(there, arrived, held), jnp.where(there, held, arrived)], axis=0
        )
    held = jnp.broadcast_to(held[None], (near, *held.shape))
    gathered = [lax.all_to_all(held, "op", 0, 0, axis_index_groups=groups)]
    for away in range(1, sec_devices):
        turn = [(i, (i + away) % sec_devices) for i in range(sec_devices)]
        gathered.append(lax.ppermute(gathered[0], "sec", turn))
    own = pl.pallas_call(
        functools.partial(in_order, blocks, left_rows // op_devices),
        out_shape=jax.ShapeDtypeStruct((order, order), BF16),
        in_specs=[VMEM],
        out_specs=VMEM,
        compiler_params=pltpu.CompilerParams(vmem_limit_bytes=2**20),
        cost_estimate=costs(4 * slots * left_rows * order),
    )(gathered[0])

    summed = pl.pallas_call(
        functools.partial(terms_kernel, blocks),
        out_shape=jax.ShapeDtypeStruct((near, left_rows // near, order), BF16),
        in_specs=[SMEM, VMEM, HBM] + [VMEM] * sec_devices,
        out_specs=VMEM,
        scratch_shapes=[
            pltpu.VMEM((sec_devices, order, order), BF16),
            pltpu.VMEM(right_ops.shape, BF16),
            pltpu.SemaphoreType.DMA((slots,)),
        ],
        compiler_params=pltpu.CompilerParams(vmem_limit_bytes=49 * 2**20),
        cost_estimate=costs(4 * slots * left_rows * order, 4 * slots * left_rows * order * order),
    )(scalars, left_ops, right_ops, own, *gathered[1:])

    parts = lax.all_to_all(summed, "op", 0, 0, axis_index_groups=groups)
    keep = jnp.sum(parts.astype(F32), axis=0)
    for mask in far:
        half = keep.shape[0] // 2
        there = (op_place & mask) != 0
        send = jnp.where(there, keep[:half], keep[half:]).astype(BF16)
        keep = jnp.where(there, keep[half:], keep[:half]) + exchange(send, "op", mask).astype(F32)
    factor = (op_devices * slots) ** (-0.5)
    return (keep * factor).astype(BF16)[None]


def solution(mesh):
    placed = (
        P("sec", "op", None),
        P(("op", "sec"), None, None),
        P(("op", "sec"), None, None),
        P(("op", "sec")),
        P(),
    )
    return jax.shard_map(
        shards, mesh=mesh, in_specs=placed, out_specs=P("sec", "op", None), check_vma=False
    )
```

```python
import functools

import jax
import jax.numpy as jnp
from jax import lax
from jax.experimental import pallas as pl
from jax.experimental.pallas import tpu as pltpu
from jax.sharding import PartitionSpec as P

F32, BF16 = jnp.float32, jnp.bfloat16
SMEM = pl.BlockSpec(memory_space=pltpu.SMEM)
VMEM = pl.BlockSpec(memory_space=pltpu.VMEM)
HBM = pl.BlockSpec(memory_space=pltpu.HBM)


def exchange(value, axis, mask):
    size = lax.axis_size(axis)
    return lax.ppermute(value, axis, [(i, i ^ mask) for i in range(size)])


def spread(position, masks):
    return sum(mask for bit, mask in enumerate(masks) if position >> bit & 1)


def costs(bytes_accessed, flops=0):
    return pl.CostEstimate(flops=flops, bytes_accessed=bytes_accessed, transcendentals=0)


def load_kernel(source, place, sem):
    copy = pltpu.make_async_copy(source, place, sem)
    copy.start()
    copy.wait()


def load(array):
    return pl.pallas_call(
        load_kernel,
        out_shape=jax.ShapeDtypeStruct(array.shape, array.dtype),
        in_specs=[HBM],
        out_specs=VMEM,
        scratch_shapes=[pltpu.SemaphoreType.DMA],
        compiler_params=pltpu.CompilerParams(vmem_limit_bytes=2**20),
        cost_estimate=costs(2 * array.size * array.dtype.itemsize),
    )(array)


def in_order(order, rows, source, place):
    for position, block in enumerate(order):
        group, part = divmod(position * rows, source.shape[1])
        place[block * rows : (block + 1) * rows, :] = source[group, part : part + rows, :]


def terms_kernel(order, sector_ref, counts_ref, left_ref, right_hbm, own_ref, *refs):
    others, (sum_ref, wave, right_ref, sems) = refs[:-4], refs[-4:]
    slots, rows, sectors = left_ref.shape[0], left_ref.shape[1] // len(order), wave.shape[0]
    copies = [pltpu.make_async_copy(right_hbm.at[t], right_ref.at[t], sems.at[t]) for t in range(slots)]
    for copy in copies:
        copy.start()
    wave[0] = own_ref[...]
    for away, ref in enumerate(others):
        in_order(order, rows, ref, wave.at[away + 1])
    sector = lax.axis_index("sec")
    count = counts_ref[sector, lax.axis_index("op")]

    def halfway(slot):
        away = lax.rem(sector - sector_ref[slot] + sectors, sectors)
        product = jnp.dot(left_ref[slot], wave[away], preferred_element_type=F32).astype(BF16)
        return jnp.where(slot < count, product, jnp.zeros_like(product))

    total, ahead = None, halfway(0)
    for slot in range(slots):
        current, ahead = ahead, halfway(slot + 1) if slot + 1 < slots else None
        copies[slot].wait()
        product = lax.dot_general(
            current, right_ref[slot], (((1,), (1,)), ((), ())), preferred_element_type=F32
        )
        total = product if total is None else total + product
    for place, block in enumerate(order):
        group, part = divmod(place * rows, sum_ref.shape[1])
        sum_ref[group, part : part + rows, :] = total[block * rows : (block + 1) * rows, :].astype(BF16)


def shards(wavefunction, left_ops, right_ops, in_sector, counts):
    op_devices, sec_devices = lax.axis_size("op"), lax.axis_size("sec")
    op_place = lax.axis_index("op")
    slots, left_rows, order = left_ops.shape
    near = min(8, op_devices) if op_devices & (op_devices - 1) == 0 else op_devices
    far = [near << bit for bit in range((op_devices // near).bit_length() - 1)]
    groups = [[far_place * near + i for i in range(near)] for far_place in range(op_devices // near)]
    blocks = [i + spread(p, far[::-1]) for i in range(near) for p in range(op_devices // near)]

    held = wavefunction[0]
    for step, mask in enumerate(far[::-1]):
        arrived = exchange(held, "op", mask)
        if step == 0:
            held = load(held)
        there = (op_place & mask) != 0
        held = jnp.concatenate(
            [jnp.where(there, arrived, held), jnp.where(there, held, arrived)], axis=0
        )
    held = jnp.broadcast_to(held[None], (near, *held.shape))
    gathered = [lax.all_to_all(held, "op", 0, 0, axis_index_groups=groups)]
    for away in range(1, sec_devices):
        turn = [(i, (i + away) % sec_devices) for i in range(sec_devices)]
        gathered.append(lax.ppermute(gathered[0], "sec", turn))
    own = pl.pallas_call(
        functools.partial(in_order, blocks, left_rows // op_devices),
        out_shape=jax.ShapeDtypeStruct((order, order), BF16),
        in_specs=[VMEM],
        out_specs=VMEM,
        compiler_params=pltpu.CompilerParams(vmem_limit_bytes=2**20),
        cost_estimate=costs(4 * slots * left_rows * order),
    )(gathered[0])

    summed = pl.pallas_call(
        functools.partial(terms_kernel, blocks),
        out_shape=jax.ShapeDtypeStruct((near, left_rows // near, order), BF16),
        in_specs=[SMEM, SMEM, VMEM, HBM] + [VMEM] * sec_devices,
        out_specs=VMEM,
        scratch_shapes=[
            pltpu.VMEM((sec_devices, order, order), BF16),
            pltpu.VMEM(right_ops.shape, BF16),
            pltpu.SemaphoreType.DMA((slots,)),
        ],
        compiler_params=pltpu.CompilerParams(vmem_limit_bytes=49 * 2**20),
        cost_estimate=costs(4 * slots * left_rows * order, 4 * slots * left_rows * order * order),
    )(in_sector, counts.T, left_ops, right_ops, own, *gathered[1:])

    parts = lax.all_to_all(summed, "op", 0, 0, axis_index_groups=groups)
    keep = jnp.sum(parts.astype(F32), axis=0)
    for mask in far:
        half = keep.shape[0] // 2
        there = (op_place & mask) != 0
        send = jnp.where(there, keep[:half], keep[half:]).astype(BF16)
        keep = jnp.where(there, keep[half:], keep[:half]) + exchange(send, "op", mask).astype(F32)
    factor = (op_devices * slots) ** (-0.5)
    return (keep * factor).astype(BF16)[None]


def solution(mesh):
    placed = (
        P("sec", "op", None),
        P(("op", "sec"), None, None),
        P(("op", "sec"), None, None),
        P(("op", "sec")),
        P(),
    )
    return jax.shard_map(
        shards, mesh=mesh, in_specs=placed, out_specs=P("sec", "op", None), check_vma=False
    )
```

```python
import functools

import jax
import jax.numpy as jnp
from jax import lax
from jax.experimental import pallas as pl
from jax.experimental.pallas import tpu as pltpu
from jax.sharding import PartitionSpec as P

F32, BF16 = jnp.float32, jnp.bfloat16
SMEM = pl.BlockSpec(memory_space=pltpu.SMEM)
VMEM = pl.BlockSpec(memory_space=pltpu.VMEM)
HBM = pl.BlockSpec(memory_space=pltpu.HBM)
GATHER_NEAR, SCATTER_NEAR = 8, 8
READY_LIMIT = 49 * 2**20


def exchange(value, axis, mask):
    size = lax.axis_size(axis)
    return lax.ppermute(value, axis, [(i, i ^ mask) for i in range(size)])


def spread(position, masks):
    return sum(mask for bit, mask in enumerate(masks) if position >> bit & 1)


def costs(bytes_accessed, flops=0):
    return pl.CostEstimate(flops=flops, bytes_accessed=bytes_accessed, transcendentals=0)


def load_kernel(source, place, sem):
    copy = pltpu.make_async_copy(source, place, sem)
    copy.start()
    copy.wait()


def load(array):
    return pl.pallas_call(
        load_kernel,
        out_shape=jax.ShapeDtypeStruct(array.shape, array.dtype),
        in_specs=[HBM],
        out_specs=VMEM,
        scratch_shapes=[pltpu.SemaphoreType.DMA],
        compiler_params=pltpu.CompilerParams(vmem_limit_bytes=2**20),
        cost_estimate=costs(2 * array.size * array.dtype.itemsize),
    )(array)


def in_order(order, rows, source, place):
    for position, block in enumerate(order):
        group, part = divmod(position * rows, source.shape[1])
        place[block * rows : (block + 1) * rows, :] = source[group, part : part + rows, :]


def ready_kernel(order, right_hbm, source, right_ref, own_ref, sem):
    copy = pltpu.make_async_copy(right_hbm, right_ref, sem)
    copy.start()
    in_order(order, own_ref.shape[0] // len(order), source, own_ref)
    copy.wait()


def terms_kernel(order, sum_order, sector_ref, counts_ref, left_ref, right_ref, own_ref, *refs):
    others, (sum_ref, wave) = refs[:-2], refs[-2:]
    slots, rows, sectors = left_ref.shape[0], left_ref.shape[1] // len(order), wave.shape[0]
    wave[0] = own_ref[...]
    for away, ref in enumerate(others):
        in_order(order, rows, ref, wave.at[away + 1])
    sector = lax.axis_index("sec")
    count = counts_ref[sector, lax.axis_index("op")]
    total = None
    for slot in range(slots):
        away = lax.rem(sector - sector_ref[slot] + sectors, sectors)
        halfway = jnp.dot(left_ref[slot], wave[away], preferred_element_type=F32).astype(BF16)
        halfway = jnp.where(slot < count, halfway, jnp.zeros_like(halfway))
        product = lax.dot_general(
            halfway, right_ref[slot], (((1,), (1,)), ((), ())), preferred_element_type=F32
        )
        total = product if total is None else total + product
    for place, block in enumerate(sum_order):
        group, part = divmod(place * rows, sum_ref.shape[1])
        sum_ref[group, part : part + rows, :] = total[block * rows : (block + 1) * rows, :].astype(BF16)


def shards(wavefunction, left_ops, right_ops, in_sector, counts):
    op_devices, sec_devices = lax.axis_size("op"), lax.axis_size("sec")
    op_place = lax.axis_index("op")
    slots, left_rows, order = left_ops.shape
    def split(near):
        if op_devices & (op_devices - 1):
            near = op_devices
        near = min(near, op_devices)
        far = [near << bit for bit in range((op_devices // near).bit_length() - 1)]
        groups = [[place * near + i for i in range(near)] for place in range(op_devices // near)]
        blocks = [i + spread(p, far[::-1]) for i in range(near) for p in range(op_devices // near)]
        return near, far, groups, blocks

    near, far, groups, blocks = split(GATHER_NEAR)
    held = wavefunction[0]
    for step, mask in enumerate(far[::-1]):
        arrived = exchange(held, "op", mask)
        if step == 0:
            held = load(held)
        there = (op_place & mask) != 0
        held = jnp.concatenate(
            [jnp.where(there, arrived, held), jnp.where(there, held, arrived)], axis=0
        )
    held = jnp.broadcast_to(held[None], (near, *held.shape))
    gathered = [lax.all_to_all(held, "op", 0, 0, axis_index_groups=groups)]
    for away in range(1, sec_devices):
        turn = [(i, (i + away) % sec_devices) for i in range(sec_devices)]
        gathered.append(lax.ppermute(gathered[0], "sec", turn))
    right, own = pl.pallas_call(
        functools.partial(ready_kernel, blocks),
        out_shape=(
            jax.ShapeDtypeStruct(right_ops.shape, BF16),
            jax.ShapeDtypeStruct((order, order), BF16),
        ),
        in_specs=[HBM, VMEM],
        out_specs=(VMEM, VMEM),
        scratch_shapes=[pltpu.SemaphoreType.DMA],
        compiler_params=pltpu.CompilerParams(vmem_limit_bytes=READY_LIMIT),
        cost_estimate=costs(4 * slots * left_rows * order),
    )(right_ops, gathered[0])

    near, far, groups, sum_blocks = split(SCATTER_NEAR)
    summed = pl.pallas_call(
        functools.partial(terms_kernel, blocks, sum_blocks),
        out_shape=jax.ShapeDtypeStruct((near, left_rows // near, order), BF16),
        in_specs=[SMEM] * 2 + [VMEM] * (2 + sec_devices),
        out_specs=VMEM,
        scratch_shapes=[pltpu.VMEM((sec_devices, order, order), BF16)],
        compiler_params=pltpu.CompilerParams(vmem_limit_bytes=16 * 2**20),
        cost_estimate=costs(4 * slots * left_rows * order, 4 * slots * left_rows * order * order),
    )(in_sector, counts.T, left_ops, right, own, *gathered[1:])

    parts = lax.all_to_all(summed, "op", 0, 0, axis_index_groups=groups)
    keep = jnp.sum(parts.astype(F32), axis=0)
    for mask in far:
        half = keep.shape[0] // 2
        there = (op_place & mask) != 0
        send = jnp.where(there, keep[:half], keep[half:]).astype(BF16)
        keep = jnp.where(there, keep[half:], keep[:half]) + exchange(send, "op", mask).astype(F32)
    factor = (op_devices * slots) ** (-0.5)
    return (keep * factor).astype(BF16)[None]


def solution(mesh):
    placed = (
        P("sec", "op", None),
        P(("op", "sec"), None, None),
        P(("op", "sec"), None, None),
        P(("op", "sec")),
        P(),
    )
    return jax.shard_map(
        shards, mesh=mesh, in_specs=placed, out_specs=P("sec", "op", None), check_vma=False
    )
```

```python
import functools

import jax
import jax.numpy as jnp
from jax import lax
from jax.experimental import pallas as pl
from jax.experimental.pallas import tpu as pltpu
from jax.sharding import PartitionSpec as P

F32, BF16 = jnp.float32, jnp.bfloat16
SMEM = pl.BlockSpec(memory_space=pltpu.SMEM)
VMEM = pl.BlockSpec(memory_space=pltpu.VMEM)
HBM = pl.BlockSpec(memory_space=pltpu.HBM)
NEAR_ORDER = (0, 7, 5, 3, 1, 6, 4, 2)
READY_LIMIT = 49 * 2**20


def exchange(value, axis, mask):
    size = lax.axis_size(axis)
    return lax.ppermute(value, axis, [(i, i ^ mask) for i in range(size)])


def spread(position, masks):
    return sum(mask for bit, mask in enumerate(masks) if position >> bit & 1)


def costs(bytes_accessed, flops=0):
    return pl.CostEstimate(flops=flops, bytes_accessed=bytes_accessed, transcendentals=0)


def load_kernel(source, place, sem):
    copy = pltpu.make_async_copy(source, place, sem)
    copy.start()
    copy.wait()


def load(array):
    return pl.pallas_call(
        load_kernel,
        out_shape=jax.ShapeDtypeStruct(array.shape, array.dtype),
        in_specs=[HBM],
        out_specs=VMEM,
        scratch_shapes=[pltpu.SemaphoreType.DMA],
        compiler_params=pltpu.CompilerParams(vmem_limit_bytes=2**20),
        cost_estimate=costs(2 * array.size * array.dtype.itemsize),
    )(array)


def in_order(order, rows, source, place):
    for position, block in enumerate(order):
        group, part = divmod(position * rows, source.shape[1])
        place[block * rows : (block + 1) * rows, :] = source[group, part : part + rows, :]


def ready_kernel(order, right_hbm, source, right_ref, own_ref, sem):
    copy = pltpu.make_async_copy(right_hbm, right_ref, sem)
    copy.start()
    in_order(order, own_ref.shape[0] // len(order), source, own_ref)
    copy.wait()


def terms_kernel(order, sector_ref, counts_ref, left_ref, right_ref, own_ref, *refs):
    others, (sum_ref, wave) = refs[:-2], refs[-2:]
    slots, rows, sectors = left_ref.shape[0], left_ref.shape[1] // len(order), wave.shape[0]
    wave[0] = own_ref[...]
    for away, ref in enumerate(others):
        in_order(order, rows, ref, wave.at[away + 1])
    sector = lax.axis_index("sec")
    count = counts_ref[sector, lax.axis_index("op")]
    total = None
    for slot in range(slots):
        away = lax.rem(sector - sector_ref[slot] + sectors, sectors)
        halfway = jnp.dot(left_ref[slot], wave[away], preferred_element_type=F32).astype(BF16)
        halfway = jnp.where(slot < count, halfway, jnp.zeros_like(halfway))
        product = lax.dot_general(
            halfway, right_ref[slot], (((1,), (1,)), ((), ())), preferred_element_type=F32
        )
        total = product if total is None else total + product
    for place, block in enumerate(order):
        group, part = divmod(place * rows, sum_ref.shape[1])
        sum_ref[group, part : part + rows, :] = total[block * rows : (block + 1) * rows, :].astype(BF16)


def shards(wavefunction, left_ops, right_ops, in_sector, counts):
    op_devices, sec_devices = lax.axis_size("op"), lax.axis_size("sec")
    op_place = lax.axis_index("op")
    slots, left_rows, order = left_ops.shape
    ring = NEAR_ORDER if op_devices % 8 == 0 and op_devices & (op_devices - 1) == 0 else range(op_devices)
    near = len(ring)
    far = [near << bit for bit in range((op_devices // near).bit_length() - 1)]
    groups = [[place * near + i for i in ring] for place in range(op_devices // near)]
    blocks = [i + spread(p, far[::-1]) for i in ring for p in range(op_devices // near)]

    held = wavefunction[0]
    for step, mask in enumerate(far[::-1]):
        arrived = exchange(held, "op", mask)
        if step == 0:
            held = load(held)
        there = (op_place & mask) != 0
        held = jnp.concatenate(
            [jnp.where(there, arrived, held), jnp.where(there, held, arrived)], axis=0
        )
    held = jnp.broadcast_to(held[None], (near, *held.shape))
    gathered = [lax.all_to_all(held, "op", 0, 0, axis_index_groups=groups)]
    for away in range(1, sec_devices):
        turn = [(i, (i + away) % sec_devices) for i in range(sec_devices)]
        gathered.append(lax.ppermute(gathered[0], "sec", turn))
    right, own = pl.pallas_call(
        functools.partial(ready_kernel, blocks),
        out_shape=(
            jax.ShapeDtypeStruct(right_ops.shape, BF16),
            jax.ShapeDtypeStruct((order, order), BF16),
        ),
        in_specs=[HBM, VMEM],
        out_specs=(VMEM, VMEM),
        scratch_shapes=[pltpu.SemaphoreType.DMA],
        compiler_params=pltpu.CompilerParams(vmem_limit_bytes=READY_LIMIT),
        cost_estimate=costs(4 * slots * left_rows * order),
    )(right_ops, gathered[0])

    summed = pl.pallas_call(
        functools.partial(terms_kernel, blocks),
        out_shape=jax.ShapeDtypeStruct((near, left_rows // near, order), BF16),
        in_specs=[SMEM] * 2 + [VMEM] * (2 + sec_devices),
        out_specs=VMEM,
        scratch_shapes=[pltpu.VMEM((sec_devices, order, order), BF16)],
        compiler_params=pltpu.CompilerParams(vmem_limit_bytes=16 * 2**20),
        cost_estimate=costs(4 * slots * left_rows * order, 4 * slots * left_rows * order * order),
    )(in_sector, counts.T, left_ops, right, own, *gathered[1:])

    parts = lax.all_to_all(summed, "op", 0, 0, axis_index_groups=groups)
    keep = jnp.sum(parts.astype(F32), axis=0)
    for mask in far:
        half = keep.shape[0] // 2
        there = (op_place & mask) != 0
        send = jnp.where(there, keep[:half], keep[half:]).astype(BF16)
        keep = jnp.where(there, keep[half:], keep[:half]) + exchange(send, "op", mask).astype(F32)
    factor = (op_devices * slots) ** (-0.5)
    return (keep * factor).astype(BF16)[None]


def solution(mesh):
    placed = (
        P("sec", "op", None),
        P(("op", "sec"), None, None),
        P(("op", "sec"), None, None),
        P(("op", "sec")),
        P(),
    )
    return jax.shard_map(
        shards, mesh=mesh, in_specs=placed, out_specs=P("sec", "op", None), check_vma=False
    )
```

```python
import functools

import jax
import jax.numpy as jnp
from jax import lax
from jax.experimental import pallas as pl
from jax.experimental.pallas import tpu as pltpu
from jax.sharding import PartitionSpec as P

F32, BF16 = jnp.float32, jnp.bfloat16
SMEM = pl.BlockSpec(memory_space=pltpu.SMEM)
VMEM = pl.BlockSpec(memory_space=pltpu.VMEM)
HBM = pl.BlockSpec(memory_space=pltpu.HBM)
NEAR_ORDER = (0, 7, 5, 3, 1, 6, 4, 2)
READY_LIMIT = 46 * 2**20


def exchange(value, axis, mask):
    size = lax.axis_size(axis)
    return lax.ppermute(value, axis, [(i, i ^ mask) for i in range(size)])


def spread(position, masks):
    return sum(mask for bit, mask in enumerate(masks) if position >> bit & 1)


def costs(bytes_accessed, flops=0):
    return pl.CostEstimate(flops=flops, bytes_accessed=bytes_accessed, transcendentals=0)


def load_kernel(source, place, sem):
    copy = pltpu.make_async_copy(source, place, sem)
    copy.start()
    copy.wait()


def load(array):
    return pl.pallas_call(
        load_kernel,
        out_shape=jax.ShapeDtypeStruct(array.shape, array.dtype),
        in_specs=[HBM],
        out_specs=VMEM,
        scratch_shapes=[pltpu.SemaphoreType.DMA],
        compiler_params=pltpu.CompilerParams(vmem_limit_bytes=2**20),
        cost_estimate=costs(2 * array.size * array.dtype.itemsize),
    )(array)


def in_order(order, rows, source, place):
    for position, block in enumerate(order):
        group, part = divmod(position * rows, source.shape[1])
        place[block * rows : (block + 1) * rows, :] = source[group, part : part + rows, :]


def distance(slot, sector_ref, counts_ref, sectors):
    sector = lax.axis_index("sec")
    away = lax.rem(sector - sector_ref[slot] + sectors, sectors)
    return jnp.where(slot < counts_ref[sector, lax.axis_index("op")], away, -1)


def ready_kernel(sectors, sector_ref, counts_ref, left_ref, right_hbm, own, right_ref, halfway_ref, sem):
    copy = pltpu.make_async_copy(right_hbm, right_ref, sem)
    copy.start()
    for slot in range(left_ref.shape[0]):
        halfway = jnp.dot(left_ref[slot], own[...], preferred_element_type=F32).astype(BF16)
        is_own = distance(slot, sector_ref, counts_ref, sectors) == 0
        halfway_ref[slot] = jnp.where(is_own, halfway, jnp.zeros_like(halfway))
    copy.wait()


def terms_kernel(order, sector_ref, counts_ref, left_ref, right_ref, own_ref, *refs):
    others, (sum_ref, wave, halfways) = refs[:-3], refs[-3:]
    slots, rows = left_ref.shape[0], left_ref.shape[1] // len(order)
    for away, ref in enumerate(others):
        in_order(order, rows, ref, wave.at[away])
    for slot in range(slots):
        away = distance(slot, sector_ref, counts_ref, len(others) + 1)

        @pl.when(away > 0)
        def _():
            other = wave[jnp.maximum(away - 1, 0)]
            halfways[slot] = jnp.dot(left_ref[slot], other, preferred_element_type=F32).astype(BF16)

        @pl.when(away <= 0)
        def _():
            halfways[slot] = own_ref[slot]

    total = None
    for slot in range(slots):
        product = lax.dot_general(
            halfways[slot], right_ref[slot], (((1,), (1,)), ((), ())), preferred_element_type=F32
        )
        total = product if total is None else total + product
    for place, block in enumerate(order):
        group, part = divmod(place * rows, sum_ref.shape[1])
        sum_ref[group, part : part + rows, :] = total[block * rows : (block + 1) * rows, :].astype(BF16)


def shards(wavefunction, left_ops, right_ops, in_sector, counts):
    op_devices, sec_devices = lax.axis_size("op"), lax.axis_size("sec")
    op_place = lax.axis_index("op")
    slots, left_rows, order = left_ops.shape
    ring = NEAR_ORDER if op_devices % 8 == 0 and op_devices & (op_devices - 1) == 0 else range(op_devices)
    near = len(ring)
    far = [near << bit for bit in range((op_devices // near).bit_length() - 1)]
    groups = [[place * near + i for i in ring] for place in range(op_devices // near)]
    blocks = [i + spread(p, far[::-1]) for i in ring for p in range(op_devices // near)]

    held = wavefunction[0]
    for step, mask in enumerate(far[::-1]):
        arrived = exchange(held, "op", mask)
        if step == 0:
            held = load(held)
        there = (op_place & mask) != 0
        held = jnp.concatenate(
            [jnp.where(there, arrived, held), jnp.where(there, held, arrived)], axis=0
        )
    held = jnp.broadcast_to(held[None], (near, *held.shape))
    gathered = [lax.all_to_all(held, "op", 0, 0, axis_index_groups=groups)]
    for away in range(1, sec_devices):
        turn = [(i, (i + away) % sec_devices) for i in range(sec_devices)]
        gathered.append(lax.ppermute(gathered[0], "sec", turn))
    ordered = pl.pallas_call(
        functools.partial(in_order, blocks, left_rows // op_devices),
        out_shape=jax.ShapeDtypeStruct((order, order), BF16),
        in_specs=[VMEM],
        out_specs=VMEM,
        compiler_params=pltpu.CompilerParams(vmem_limit_bytes=2**20),
        cost_estimate=costs(4 * order * order),
    )(gathered[0])
    halfway = jax.ShapeDtypeStruct((slots, left_rows, order), BF16)
    right, own = pl.pallas_call(
        functools.partial(ready_kernel, sec_devices),
        out_shape=(jax.ShapeDtypeStruct(right_ops.shape, BF16), halfway),
        in_specs=[SMEM, SMEM, VMEM, HBM, VMEM],
        out_specs=(VMEM, VMEM),
        scratch_shapes=[pltpu.SemaphoreType.DMA],
        compiler_params=pltpu.CompilerParams(vmem_limit_bytes=READY_LIMIT),
        cost_estimate=costs(4 * slots * left_rows * order),
    )(in_sector, counts.T, left_ops, right_ops, ordered)

    summed = pl.pallas_call(
        functools.partial(terms_kernel, blocks),
        out_shape=jax.ShapeDtypeStruct((near, left_rows // near, order), BF16),
        in_specs=[SMEM] * 2 + [VMEM] * (2 + sec_devices),
        out_specs=VMEM,
        scratch_shapes=[
            pltpu.VMEM((max(sec_devices - 1, 1), order, order), BF16),
            pltpu.VMEM(halfway.shape, BF16),
        ],
        compiler_params=pltpu.CompilerParams(vmem_limit_bytes=16 * 2**20),
        cost_estimate=costs(4 * slots * left_rows * order, 4 * slots * left_rows * order * order),
    )(in_sector, counts.T, left_ops, right, own, *gathered[1:])

    parts = lax.all_to_all(summed, "op", 0, 0, axis_index_groups=groups)
    keep = jnp.sum(parts.astype(F32), axis=0)
    for mask in far:
        half = keep.shape[0] // 2
        there = (op_place & mask) != 0
        send = jnp.where(there, keep[:half], keep[half:]).astype(BF16)
        keep = jnp.where(there, keep[half:], keep[:half]) + exchange(send, "op", mask).astype(F32)
    factor = (op_devices * slots) ** (-0.5)
    return (keep * factor).astype(BF16)[None]


def solution(mesh):
    placed = (
        P("sec", "op", None),
        P(("op", "sec"), None, None),
        P(("op", "sec"), None, None),
        P(("op", "sec")),
        P(),
    )
    return jax.shard_map(
        shards, mesh=mesh, in_specs=placed, out_specs=P("sec", "op", None), check_vma=False
    )
```
